256 devices in a mesh: band: 64 (over z, x, core), patch: 4 (over y).
Axes of the slice: x: 4, y: 4, z: 8, core: 2. Of those that a mesh axis runs over, the one named last changes fastest.
Arguments:
- grid_feat: bfloat16 [524288, 512], P(('band', 'patch')), may hold values from -6 to 6
- mesh_feat: bfloat16 [65536, 512], P(('band', 'patch')), may hold values from -6 to 6
- grid_band: int32 [524288, 1], P(('band', 'patch')), may hold values from 0 to 63; in each aligned block of 2048 rows (0 to 2047, 2048 to 4095, ...) at most 64 rows name the same one
- grid_target: int32 [524288], P(('band', 'patch')), may hold values from 0 to 255
- mesh_nbr: int32 [65536, 6], P(('band', 'patch')), may hold values from 0 to 383
- w_in: bfloat16 [512, 512], replicated, may hold values from -0.25 to 0.25
- w_mesh: bfloat16 [512, 512], replicated, may hold values from -0.25 to 0.25
- w_edge: bfloat16 [512, 512], replicated, may hold values from -0.25 to 0.25
- w_out: bfloat16 [512, 512], replicated, may hold values from -0.1875 to 0.1875
- cotangent: bfloat16 [65536, 512], P(('band', 'patch')), may hold values from -6 to 6
Outputs:
- mesh_out: bfloat16 [65536, 512], P(('band', 'patch'))
- mesh_grad: bfloat16 [65536, 512], P(('band', 'patch'))
- grid_grad: bfloat16 [524288, 512], P(('band', 'patch'))
The draws below stay inside these ranges and needn't reach their ends.
Inputs may be any that keep to these rules, and one draw needn't show every extreme that they name: `grid_band`: among the grid rows of one device at most 64 name the same band, and on some device one band is named by exactly 64 of them.
All inputs are finite; a program needn't handle non-finite values.
Results may differ from the reference program's by a relative error of at most 0.015.
Values may be sent and summed in bfloat16 or wider, within the bound.
No kernel may reach another device: no remote copies, remote signals or barrier semaphores. Data moves between devices by JAX's collectives and lax.ppermute only.
A program may use at most 64 MiB of HBM per device.

```python
import math
import jax
import jax.numpy as jnp
import numpy as np

D = 512
G_DEV = 2048
M_DEV = 256
HALO = 64
NBRS = 6
CAP = 64
GRID = 524288
MESH = 65536
N_BAND = 64
N_PATCH = 4


def touch_ends(result, own_key, smallest, high):
    longest = result.shape.index(max(result.shape))
    spots = []
    for shift in (0, 1):
        where = [jax.random.randint(jax.random.fold_in(own_key, axis), (), 0, length) for axis, length in enumerate(result.shape)]
        where[longest] = (where[longest] + shift) % result.shape[longest]
        spots.append(tuple(where))
    return result.at[spots[0]].set(smallest).at[spots[1]].set(high)


def level_of(stream_key, extent, shards, least, high):
    level, own = 1.0, jax.random.fold_in(stream_key, 6)
    for dim, blocks in shards:
        draws = jnp.exp(jax.random.uniform(jax.random.fold_in(own, dim), (blocks,), jnp.float32, least / len(shards), high / len(shards)))
        level = level * jnp.repeat(draws, extent[dim] // blocks).reshape([-1 if axis == dim else 1 for axis in range(len(extent))])
    return level


def shared_out(rng, own, number, rows, number_of, top, bound, lean):
    order = jax.random.permutation(rng, number_of)
    crowded, usual = portions_of(number_of, rows * top, bound, lean, True), portions_of(number_of, rows * top, bound, lean, False)
    places = jnp.arange(number_of)

    def named(sizes, turn):
        used = int((sizes > 0).sum())
        fixed = max(1, used // 4)
        passed = fixed + (places - fixed + turn * (used - fixed)) % max(1, number_of - fixed)
        return jnp.zeros((number_of,), jnp.int32).at[order[jnp.where(places < fixed, places, passed)]].set(jnp.asarray(sizes, jnp.int32))

    sizes = jnp.where(number % 4 == 0, named(crowded, number // 4), named(usual, number - number // 4 - 1))
    mixed = jax.random.permutation(jax.random.fold_in(own, 3), number_of)
    giver, receiver = mixed[0:number_of // 2 * 2:2], mixed[1:number_of // 2 * 2:2]
    margin = jnp.minimum(sizes[giver] - 1, bound - sizes[receiver]) // 2
    margin = jnp.where((giver == order[0]) | (receiver == order[0]) | (sizes[receiver] == 0), 0, jnp.maximum(margin, 0))
    passed = jax.random.randint(jax.random.fold_in(own, 4), (number_of // 2,), 0, 1 << 20) % (margin + 1)
    sizes = sizes.at[giver].add(-passed).at[receiver].add(passed)
    labels = jnp.searchsorted(jnp.cumsum(sizes), jnp.arange(rows * top), side="right").astype(jnp.int32)
    table = labels.reshape(top, rows).T
    table = table[jax.random.permutation(jax.random.fold_in(own, 1), rows)]
    turn = jax.random.randint(jax.random.fold_in(own, 2), (rows, 1), 0, top)
    return jnp.take_along_axis(table, (jnp.arange(top)[None, :] + turn) % top, axis=1)


def portions_of(count, total, bound, lean, full):
    loads = [(1 << 20) // math.isqrt(standing ** lean) + 1 for standing in range(1, count + 1)]
    largest = bound if full else min(bound, max(-(-total // count), total * loads[0] // sum(loads)))
    least = 1 if total - largest >= count - 1 else 0
    counts, spare = [largest] + [least] * (count - 1), total - largest - least * (count - 1)
    while spare > 0:
        free = [i for i in range(1, count) if counts[i] < largest] or [i for i in range(1, count) if counts[i] < bound]
        pool, budget = sum([loads[i] for i in free]), spare
        for i in free:
            more = min(bound - counts[i], max(1, budget * loads[i] // pool), spare)
            counts[i] = counts[i] + more
            spare = spare - more
    return np.array(counts)


def scatter_about(key, dims, deviation, limit, cuts=(), held_as=jnp.bfloat16):
    factor_of = level_of(key, dims, cuts, -0.22, 0.18) if cuts else 1.0
    values = jax.random.normal(key, dims, jnp.float32) * deviation * factor_of
    return jnp.minimum(jnp.maximum(values, -limit), limit).astype(held_as)


def setup_inputs(seed: int = 0) -> dict:
    key_list = jax.random.split(jax.random.key(seed), 11)
    grid_feat = scatter_about(key_list[0], (GRID, D), 1.0, 6.0, ((0, 256),))
    mesh_feat = scatter_about(key_list[1], (MESH, D), 1.0, 6.0, ((0, 256),))
    grid_band_keys = jax.random.split(jax.random.fold_in(key_list[2], 1), GRID // G_DEV)
    grid_band_turns = jax.random.permutation(jax.random.fold_in(key_list[2], 3), GRID // G_DEV)
    grid_band = jax.vmap(lambda own, number: shared_out(jax.random.fold_in(key_list[2], 2), own, number, G_DEV, N_BAND, 1, CAP, 2))(grid_band_keys, grid_band_turns).reshape((GRID, 1))
    grid_target = touch_ends(jax.random.randint(key_list[3], (GRID,), 0, M_DEV), jax.random.fold_in(key_list[3], 1), 0, M_DEV - 1).astype(jnp.int32)
    mesh_nbr = touch_ends(jax.random.randint(key_list[4], (MESH, NBRS), 0, M_DEV + 2 * HALO), jax.random.fold_in(key_list[4], 1), 0, (M_DEV + 2 * HALO) - 1).astype(jnp.int32)
    w_in = scatter_about(key_list[5], (D, D), D ** -0.5, 0.25)
    w_mesh = scatter_about(key_list[6], (D, D), D ** -0.5, 0.25)
    w_edge = scatter_about(key_list[7], (D, D), D ** -0.5, 0.25)
    w_out = scatter_about(key_list[8], (D, D), (2 * D) ** -0.5, 0.1875)
    cotangent = scatter_about(key_list[9], (MESH, D), 1.0, 6.0, ((0, 256),))
    return dict(grid_feat=grid_feat, mesh_feat=mesh_feat, grid_band=grid_band, grid_target=grid_target, mesh_nbr=mesh_nbr, w_in=w_in, w_mesh=w_mesh, w_edge=w_edge, w_out=w_out, cotangent=cotangent)


def silu_slope(values):
    sigma = jax.nn.sigmoid(values)
    return sigma * (1.0 + values * (1.0 - sigma))


def reference(grid_feat, mesh_feat, grid_band, grid_target, mesh_nbr, w_in, w_mesh, w_edge, w_out, cotangent):
    pre_in = jnp.dot(grid_feat, w_in, preferred_element_type=jnp.float32)
    message = jax.nn.silu(pre_in).astype(jnp.bfloat16)
    grid_index = jnp.arange(GRID, dtype=jnp.int32)
    grid_patch = (grid_index // G_DEV) % N_PATCH
    node_index = ((grid_band[:, 0] * N_PATCH + grid_patch) * M_DEV + grid_target).astype(jnp.int32)
    gathered = jax.ops.segment_sum(message.astype(jnp.float32), node_index, num_segments=MESH).astype(jnp.bfloat16)
    pre_mesh = jnp.dot(gathered, w_mesh, preferred_element_type=jnp.float32)
    latent = (mesh_feat.astype(jnp.float32) + jax.nn.silu(pre_mesh)).astype(jnp.bfloat16)
    pre_edge = jnp.dot(latent, w_edge, preferred_element_type=jnp.float32)
    sender = jax.nn.silu(pre_edge).astype(jnp.bfloat16)
    mesh_index = jnp.arange(MESH, dtype=jnp.int32)
    mesh_device = mesh_index // M_DEV
    band_of = (mesh_device // N_PATCH)[:, None]
    patch_of = (mesh_device % N_PATCH)[:, None]
    to_left = mesh_nbr < HALO
    to_right = mesh_nbr >= M_DEV + HALO
    source_patch = jnp.where(to_left, (patch_of - 1) % N_PATCH, jnp.where(to_right, (patch_of + 1) % N_PATCH, patch_of))
    source_row = jnp.where(to_left, M_DEV - HALO + mesh_nbr, jnp.where(to_right, mesh_nbr - M_DEV - HALO, mesh_nbr - HALO))
    source = ((band_of * N_PATCH + source_patch) * M_DEV + source_row).astype(jnp.int32)
    edge_total = jnp.zeros((MESH, D), jnp.float32)
    for column in range(NBRS):
        edge_total = edge_total + sender[source[:, column]].astype(jnp.float32)
    edge_low = edge_total.astype(jnp.bfloat16)
    mesh_out = (latent.astype(jnp.float32) + jnp.dot(edge_low, w_out, preferred_element_type=jnp.float32)).astype(jnp.bfloat16)
    d_edge = jnp.dot(cotangent, w_out.T, preferred_element_type=jnp.float32).astype(jnp.bfloat16)
    d_sender = jnp.zeros((MESH, D), jnp.float32)
    for column in range(NBRS):
        d_sender = d_sender.at[source[:, column]].add(d_edge.astype(jnp.float32))
    d_pre_edge = (d_sender * silu_slope(pre_edge)).astype(jnp.bfloat16)
    d_latent = cotangent.astype(jnp.float32) + jnp.dot(d_pre_edge, w_edge.T, preferred_element_type=jnp.float32)
    mesh_grad = d_latent.astype(jnp.bfloat16)
    d_pre_mesh = (d_latent * silu_slope(pre_mesh)).astype(jnp.bfloat16)
    d_gathered = jnp.dot(d_pre_mesh, w_mesh.T, preferred_element_type=jnp.float32).astype(jnp.bfloat16)
    d_message = d_gathered[node_index]
    d_pre_in = (d_message.astype(jnp.float32) * silu_slope(pre_in)).astype(jnp.bfloat16)
    grid_grad = jnp.dot(d_pre_in, w_in.T, preferred_element_type=jnp.float32).astype(jnp.bfloat16)
    return (mesh_out, mesh_grad, grid_grad)
```

```python
import functools

import jax
import jax.numpy as jnp
from jax import lax
from jax.experimental import pallas as pl
from jax.experimental.pallas import tpu as pltpu
from jax.sharding import PartitionSpec as P

HALO = 64
NZ = 8
NX = 4
CAP = 64
CHUNKS = (256, 256)
F32 = jnp.float32
BF16 = jnp.bfloat16


def sigmoid(v):
    return 1.0 / (1.0 + jnp.exp(-v))


def silu_slope(v):
    s = sigmoid(v)
    return s * (1.0 + v * (1.0 - s))


def call(body, outs, *args, vmem=40, flops=0, bytes_accessed=0, **kw):
    return pl.pallas_call(
        body,
        out_shape=outs,
        compiler_params=pltpu.CompilerParams(vmem_limit_bytes=vmem * 2**20),
        cost_estimate=pl.CostEstimate(
            flops=flops, bytes_accessed=bytes_accessed, transcendentals=0
        ),
        **kw,
    )(*args)


def shape(dims, dtype=BF16):
    return jax.ShapeDtypeStruct(dims, dtype)


def dot(a, b):
    return jnp.dot(a, b, preferred_element_type=F32)


def dot_nt(a, b):
    return lax.dot_general(a, b, (((1,), (1,)), ((), ())), preferred_element_type=F32)


def index_body(q_ref, t_ref, slot_ref, table_ref):
    rows = q_ref.shape[1]
    part = 256
    below = lax.broadcasted_iota(jnp.int32, (part, part), 0)
    upper = jnp.where(below <= lax.broadcasted_iota(jnp.int32, (part, part), 1), 1.0, 0.0)
    upper = upper.astype(BF16)
    table = jnp.zeros((NX * NZ, 2 * CAP), F32)
    for side in range(2):
        carry = jnp.zeros((NX * NZ, 1), F32)
        for first in range(0, rows, part):
            here = pl.ds(first, part)
            q = q_ref[side : side + 1, here]
            hit = lax.broadcasted_iota(jnp.int32, (NX * NZ, part), 0) == q
            hits = jnp.where(hit, 1.0, 0.0)
            counted = dot(hits.astype(BF16), upper) + carry
            rank = jnp.sum(hits * counted, axis=0, keepdims=True) - 1.0
            carry = counted[:, part - 1 : part]
            rank = rank.astype(jnp.int32)
            slot_ref[side : side + 1, here] = jnp.where(q >= 0, q * CAP + rank, -1)
            named = jnp.where(hit, (t_ref[side : side + 1, here] + 1).astype(F32), 0.0)
            place = lax.broadcasted_iota(jnp.int32, (2 * CAP, part), 0) == rank + side * CAP
            table = table + dot_nt(named.astype(BF16), jnp.where(place, 1.0, 0.0).astype(BF16))
    table_ref[...] = table


def message_body(feat_ref, w_ref, *outs):
    pre = dot(feat_ref[...], w_ref[...])
    sig = sigmoid(pre)
    message = (pre * sig).astype(BF16)
    first = 0
    for index, width in enumerate(CHUNKS):
        outs[index][...] = message[:, first : first + width]
        first += width
    if len(outs) > len(CHUNKS):
        outs[-1][...] = (sig * (1.0 + pre * (1.0 - sig))).astype(BF16)


def message_of(feat, w, with_slope):
    rows, width = feat.shape
    step = 512
    widths = CHUNKS + ((width,) if with_slope else ())
    return call(
        message_body,
        [shape((rows, n)) for n in widths],
        feat,
        w,
        flops=2 * rows * width * width,
        bytes_accessed=8 * rows * width,
        grid=(rows // step,),
        in_specs=[
            pl.BlockSpec((step, width), lambda i: (i, 0)),
            pl.BlockSpec((width, width), lambda i: (0, 0)),
        ],
        out_specs=[pl.BlockSpec((step, n), lambda i: (i, 0)) for n in widths],
    )


def route_body(with_table, slot_ref, own_ref, other_ref, *rest):
    outs = rest[-NX:]
    rows = slot_ref.shape[1]
    each = NZ * CAP
    for xr in range(NX):
        for side, ref in enumerate((own_ref, other_ref)):
            place = lax.broadcasted_iota(jnp.int32, (each, rows), 0) + xr * each
            hit = place == slot_ref[side : side + 1, :]
            moved = dot(jnp.where(hit, 1.0, 0.0).astype(BF16), ref[...]).astype(BF16)
            for k in range(NZ):
                outs[xr][pl.ds((2 * k + side) * CAP, CAP), :] = moved[k * CAP : (k + 1) * CAP]
        if with_table:
            named = rest[0][pl.ds(xr * NZ, NZ), :]
            width = outs[xr].shape[1]
            tail = jnp.concatenate([named, jnp.zeros((NZ, 2 * CAP), F32)], axis=0)
            if width > 2 * CAP:
                tail = jnp.concatenate([tail, jnp.zeros((2 * NZ, width - 2 * CAP), F32)], axis=1)
            outs[xr][pl.ds(2 * each, 2 * NZ), :] = tail.astype(BF16)


def route(slot, own, other, table):
    width = own.shape[1]
    rows = 2 * NZ * CAP + (2 * NZ if table is not None else 0)
    extra = () if table is None else (table,)
    return call(
        functools.partial(route_body, table is not None),
        [shape((rows, width))] * NX,
        slot,
        own,
        other,
        *extra,
        flops=4 * 2048 * 2048 * width,
        bytes_accessed=8 * 2048 * width,
    )


def merge_body(first, *refs):
    blocks = refs[:NX]
    if first:
        near, up, down, far, two, six, table_ref, turned_ref = refs[NX:]
        for xr in range(NX):
            named = blocks[xr][pl.ds(2 * NZ * CAP, 2 * NZ), :]
            table_ref[pl.ds(xr * NZ, NZ), :] = named[:NZ, : 2 * CAP].astype(F32)
        square = jnp.concatenate(
            [table_ref[...], jnp.zeros((2 * CAP - NX * NZ, 2 * CAP), F32)], axis=0
        )
        turned_ref[...] = square.T
    else:
        table_ref = refs[NX]
        near, up, down, far, two, six = refs[NX + 1 :]
    nodes = near.shape[0]
    node = (lax.broadcasted_iota(jnp.int32, (nodes, 2 * CAP), 0) + 1).astype(F32)
    for k in range(NZ):
        total = None
        for xr in range(NX):
            hit = node == table_ref[xr * NZ + k : xr * NZ + k + 1, :]
            hits = jnp.where(hit, 1.0, 0.0).astype(BF16)
            term = dot(hits, blocks[xr][pl.ds(2 * CAP * k, 2 * CAP), :])
            total = term if total is None else total + term
        total = total.astype(BF16)
        if k == 0:
            near[...] = total
        elif k == 1:
            up[0] = total
        elif k == 3:
            up[1] = total
        elif k == 7:
            down[0] = total
        elif k == 5:
            down[1] = total
        elif k == 4:
            far[...] = total
        elif k == 2:
            two[...] = total
        else:
            six[...] = total


def merge(blocks, table, nodes):
    width = blocks[0].shape[1]
    one, both = shape((nodes, width)), shape((2, nodes, width))
    outs = [one, both, both, one, one, one]
    if table is None:
        outs += [shape((NX * NZ, 2 * CAP), F32), shape((2 * CAP, 2 * CAP), F32)]
    extra = () if table is None else (table,)
    return call(
        functools.partial(merge_body, table is None),
        outs,
        *blocks,
        *extra,
        flops=2 * NZ * NX * nodes * 2 * CAP * width,
        bytes_accessed=12 * 1024 * width,
    )


def mesh_body(*refs):
    count = len(CHUNKS)
    parts = refs[: 5 * count]
    feat, cotangent, d_sender, w_mesh, w_edge = refs[5 * count : 5 * count + 5]
    latent_ref, sender_ref, grad_ref = refs[5 * count + 5 : 5 * count + 8]
    outs = refs[5 * count + 8 :]
    pre_mesh, first = None, 0
    for index, width in enumerate(CHUNKS):
        near, up, down, two, six = parts[5 * index : 5 * index + 5]
        total = near[...].astype(F32) + up[0].astype(F32) + down[0].astype(F32)
        total = total + two[...].astype(F32) + six[...].astype(F32)
        term = dot(total.astype(BF16), w_mesh[pl.ds(first, width), :])
        pre_mesh = term if pre_mesh is None else pre_mesh + term
        first += width
    sig = sigmoid(pre_mesh)
    latent = (feat[...].astype(F32) + pre_mesh * sig).astype(BF16)
    latent_ref[...] = latent
    pre_edge = dot(latent, w_edge[...])
    edge_sig = sigmoid(pre_edge)
    sender_ref[...] = (pre_edge * edge_sig).astype(BF16)
    d_pre_edge = (d_sender[...] * (edge_sig * (1.0 + pre_edge * (1.0 - edge_sig)))).astype(BF16)
    d_latent = cotangent[...].astype(F32) + dot_nt(d_pre_edge, w_edge[...])
    grad_ref[...] = d_latent.astype(BF16)
    d_pre_mesh = (d_latent * (sig * (1.0 + pre_mesh * (1.0 - sig)))).astype(BF16)
    d_gathered = dot_nt(d_pre_mesh, w_mesh[...]).astype(BF16)
    first = 0
    for index, width in enumerate(CHUNKS):
        outs[index][...] = d_gathered[:, first : first + width]
        first += width


def expand_body(*refs):
    held, turned, outs = refs[:NZ], refs[NZ], refs[NZ + 1 :]
    nodes = held[0].shape[0]
    node = (lax.broadcasted_iota(jnp.int32, (2 * CAP, nodes), 1) + 1).astype(F32)
    for k in range(NZ):
        for xr in range(NX):
            hit = node == turned[:, xr * NZ + k : xr * NZ + k + 1]
            hits = jnp.where(hit, 1.0, 0.0).astype(BF16)
            outs[xr][pl.ds(2 * CAP * k, 2 * CAP), :] = dot(hits, held[k][...]).astype(BF16)


def expand(held, turned):
    width = held[0].shape[1]
    return call(
        expand_body,
        [shape((2 * NZ * CAP, width))] * NX,
        *held,
        turned,
        flops=2 * NZ * NX * 256 * 2 * CAP * width,
        bytes_accessed=12 * 1024 * width,
    )


def collect_body(side, *refs):
    blocks, slot_ref, out, held = refs[:NX], refs[NX], refs[NX + 1], refs[NX + 2]
    each = NZ * CAP
    for xr in range(NX):
        for k in range(NZ):
            piece = blocks[xr][pl.ds((2 * k + side) * CAP, CAP), :]
            held[pl.ds(xr * each + k * CAP, CAP), :] = piece
    rows = out.shape[0]
    step = 512
    for first in range(0, rows, step):
        here = pl.ds(first, step)
        place = lax.broadcasted_iota(jnp.int32, (step, NX * each), 1)
        hit = place == slot_ref[here, side : side + 1]
        out[here, :] = dot(jnp.where(hit, 1.0, 0.0).astype(BF16), held[...]).astype(BF16)


def collect(blocks, slot_column, side):
    width = blocks[0].shape[1]
    rows = slot_column.shape[0]
    return call(
        functools.partial(collect_body, side),
        shape((rows, width)),
        *blocks,
        slot_column,
        flops=2 * rows * NX * NZ * CAP * width,
        bytes_accessed=6 * rows * width,
        scratch_shapes=[pltpu.VMEM((NX * NZ * CAP, width), BF16)],
    )


def grid_grad_body(*refs):
    count = len(CHUNKS)
    slope, w = refs[2 * count], refs[2 * count + 1]
    out = refs[-1]
    total, first = None, 0
    for index, width in enumerate(CHUNKS):
        own, other = refs[2 * index], refs[2 * index + 1]
        d_message = own[...].astype(F32) + other[...].astype(F32)
        d_pre = d_message * slope[:, pl.ds(first, width)].astype(F32)
        term = dot_nt(d_pre.astype(BF16), w[:, pl.ds(first, width)])
        total = term if total is None else total + term
        first += width
    out[...] = total.astype(BF16)


def grid_grad_of(pieces, slope, w):
    rows, width = slope.shape
    step = 512
    flat = [piece for pair in pieces for piece in pair]
    return call(
        grid_grad_body,
        shape((rows, width)),
        *flat,
        slope,
        w,
        flops=2 * rows * width * width,
        bytes_accessed=8 * rows * width,
        grid=(rows // step,),
        in_specs=[pl.BlockSpec((step, piece.shape[1]), lambda i: (i, 0)) for piece in flat]
        + [
            pl.BlockSpec((step, width), lambda i: (i, 0)),
            pl.BlockSpec((width, width), lambda i: (0, 0)),
        ],
        out_specs=pl.BlockSpec((step, width), lambda i: (i, 0)),
    )


def band_of(z, x, core):
    return (z % NZ) * 2 * NX + (x % NX) * 2 + core


def shift(value, dz=0, dx=0, dcore=0):
    pairs = [
        (band_of(z, x, core), band_of(z + dz, x + dx, core ^ dcore))
        for z in range(NZ)
        for x in range(NX)
        for core in range(2)
    ]
    return lax.ppermute(value, "band", pairs)


def along_patch(value, by):
    size = lax.axis_size("patch")
    return lax.ppermute(value, "patch", [(i, (i + by) % size) for i in range(size)])


def local(
    grid_feat, mesh_feat, grid_band, grid_target, mesh_nbr, w_in, w_mesh, w_edge, w_out, cotangent
):
    mesh_rows, width = mesh_feat.shape
    band = lax.axis_index("band")
    here_z, here_x, here_core = band // (2 * NX), (band // 2) % NX, band % 2

    named = jnp.stack([grid_band[:, 0], grid_target])
    other_feat = shift(grid_feat, dcore=1)
    other_named = shift(named, dcore=1)
    to_band = jnp.stack([named[0], other_named[0]])
    target = jnp.stack([named[1], other_named[1]])
    zr = (to_band // (2 * NX) - here_z) % NZ
    xr = ((to_band // 2) % NX - here_x) % NX
    bucket = jnp.where(to_band % 2 == here_core, xr * NZ + zr, -1)
    rows = grid_feat.shape[0]
    slot, table = call(
        index_body, [shape((2, rows), jnp.int32), shape((NX * NZ, 2 * CAP), F32)], bucket, target
    )
    *own, slope = message_of(grid_feat, w_in, True)
    other = message_of(other_feat, w_in, False)

    span = jnp.arange(mesh_rows + 2 * HALO, dtype=jnp.int32)
    adjacency = jnp.zeros((mesh_rows, mesh_rows + 2 * HALO), F32)
    for column in range(mesh_nbr.shape[1]):
        adjacency = adjacency + (mesh_nbr[:, column : column + 1] == span[None, :]).astype(F32)
    adjacency = adjacency.astype(BF16)
    d_edge = dot(cotangent, w_out.T).astype(BF16)
    d_extended = lax.dot_general(
        adjacency, d_edge, (((0,), (0,)), ((), ())), preferred_element_type=F32
    )
    from_next = along_patch(d_extended[:HALO].astype(BF16), -1).astype(F32)
    from_prev = along_patch(d_extended[HALO + mesh_rows :].astype(BF16), 1).astype(F32)
    d_sender = d_extended[HALO : HALO + mesh_rows]
    d_sender = d_sender.at[:HALO].add(from_prev).at[mesh_rows - HALO :].add(from_next)

    parts, listed, turned = [], None, None
    for index in range(len(CHUNKS)):
        sent = route(slot, own[index], other[index], table if index == 0 else None)
        arrived = [sent[0]] + [shift(sent[k], dx=k) for k in range(1, NX)]
        merged = merge(arrived, listed, mesh_rows)
        near, up, down, far, two, six = merged[:6]
        if index == 0:
            listed, turned = merged[6:]
        up, down = shift(up, dz=1), shift(down, dz=-1)
        far_two = index % 2 == 0
        far = shift(far, dz=2 if far_two else -2)
        two = two.astype(F32) + up[1].astype(F32) + (far.astype(F32) if far_two else 0.0)
        six = six.astype(F32) + down[1].astype(F32) + (0.0 if far_two else far.astype(F32))
        two, six = shift(two.astype(BF16), dz=2), shift(six.astype(BF16), dz=-2)
        parts += [near, up, down, two, six]

    node = shape((mesh_rows, width))
    latent, sender, mesh_grad, *d_gathered = call(
        mesh_body,
        [node, node, node] + [shape((mesh_rows, n)) for n in CHUNKS],
        *parts,
        mesh_feat,
        cotangent,
        d_sender,
        w_mesh,
        w_edge,
        flops=8 * mesh_rows * width * width,
        bytes_accessed=20 * mesh_rows * width,
    )

    slot_column = slot.T
    pieces = []
    for index in range(len(CHUNKS)):
        mine = d_gathered[index]
        held = [None] * NZ
        held[0] = mine
        held[1], held[7] = shift(mine, dz=-1), shift(mine, dz=1)
        held[2], held[6] = shift(mine, dz=-2), shift(mine, dz=2)
        held[3], held[5] = shift(held[2], dz=-1), shift(held[6], dz=1)
        held[4] = shift(held[2], dz=-2) if index % 2 == 0 else shift(held[6], dz=2)
        sent = expand(held, turned)
        arrived = [sent[0]] + [shift(sent[k], dx=-k) for k in range(1, NX)]
        for_other = collect(arrived, slot_column, 1)
        from_other = shift(for_other, dcore=1)
        pieces.append((collect(arrived, slot_column, 0), from_other))
    grid_grad = grid_grad_of(pieces, slope, w_in)

    before = along_patch(sender[mesh_rows - HALO :], 1)
    after = along_patch(sender[:HALO], -1)
    extended = jnp.concatenate([before, sender, after], axis=0)
    edge_total = dot(adjacency, extended).astype(BF16)
    mesh_out = (latent.astype(F32) + dot(edge_total, w_out)).astype(BF16)
    return mesh_out, mesh_grad, grid_grad


def solution(mesh):
    spread = P(("band", "patch"), None)
    return jax.shard_map(
        local,
        mesh=mesh,
        in_specs=(
            spread,
            spread,
            spread,
            P(("band", "patch")),
            spread,
            P(),
            P(),
            P(),
            P(),
            spread,
        ),
        out_specs=(spread, spread, spread),
        check_vma=False,
    )
```

```python
import functools

import jax
import jax.numpy as jnp
from jax import lax
from jax.experimental import pallas as pl
from jax.experimental.pallas import tpu as pltpu
from jax.sharding import PartitionSpec as P

HALO = 64
NZ = 8
NX = 4
CAP = 64
FAR, MID, NEAR = (3, 4, 5), (2, 6), (1, 7, 0)
OUTER = FAR + MID
SLOT_ROWS = (
    ((0, OUTER), (1, NEAR), (7, FAR), (8, MID)),
    ((2, OUTER), (3, NEAR)),
    ((4, FAR), (5, MID), (6, NEAR)),
)
JOINED = 9
VMEM = 36 * 2**20
F32 = jnp.float32
BF16 = jnp.bfloat16


def sigmoid(v):
    return 0.5 * jnp.tanh(0.5 * v) + 0.5


def call(body, outs, *args, after=(), flops=0, bytes_accessed=0, **kw):
    if after:
        inner, count, extra = body, len(args), len(after)
        kw["in_specs"] = list(kw.get("in_specs") or [pl.BlockSpec(memory_space=pltpu.VMEM)] * count)
        kw["in_specs"] += [pl.BlockSpec(memory_space=pl.ANY)] * extra

        def body(*refs):
            inner(*refs[:count], *refs[count + extra :])

    return pl.pallas_call(
        body,
        out_shape=outs,
        compiler_params=pltpu.CompilerParams(vmem_limit_bytes=VMEM),
        cost_estimate=pl.CostEstimate(flops=0, bytes_accessed=0, transcendentals=0),
        **kw,
    )(*args, *after)


def shape(dims, dtype=BF16):
    return jax.ShapeDtypeStruct(dims, dtype)


def dot(a, b):
    return jnp.dot(a, b, preferred_element_type=F32)


def dot_nt(a, b):
    return lax.dot_general(a, b, (((1,), (1,)), ((), ())), preferred_element_type=F32)


def index_body(here_ref, own_ref, other_ref, slot_ref, table_ref):
    rows = own_ref.shape[1]
    part = 256
    below = lax.broadcasted_iota(jnp.int32, (part, part), 0)
    upper = jnp.where(below <= lax.broadcasted_iota(jnp.int32, (part, part), 1), 1.0, 0.0)
    upper = upper.astype(BF16)
    here_z, here_x, here_core = here_ref[0], here_ref[1], here_ref[2]
    table = jnp.zeros((NX * NZ, 2 * CAP), F32)
    for side, ref in enumerate((own_ref, other_ref, own_ref)):
        carry = jnp.zeros((NX * NZ, 1), F32)
        wanted = here_core if side < 2 else 1 - here_core
        for first in range(0, rows, part):
            here = pl.ds(first, part)
            band = ref[0:1, here]
            k = ((band >> 3) - here_z) & (NZ - 1)
            xr = ((band >> 1) - here_x) & (NX - 1)
            kept = (band & 1) == wanted
            q = jnp.where(kept, xr * NZ + k, -1)
            hit = lax.broadcasted_iota(jnp.int32, (NX * NZ, part), 0) == q
            hits = jnp.where(hit, 1.0, 0.0)
            counted = dot(hits.astype(BF16), upper) + carry
            rank = jnp.sum(hits * counted, axis=0, keepdims=True) - 1.0
            carry = counted[:, part - 1 : part]
            rank = rank.astype(jnp.int32)
            for row, chunk in SLOT_ROWS[side]:
                at = jnp.full_like(q, -1)
                for place, distance in enumerate(chunk):
                    at = jnp.where(k == distance, place, at)
                local = (xr * len(chunk) + at) * CAP + rank
                slot_ref[row : row + 1, here] = jnp.where(kept & (at >= 0), local, -1)
            if side < 2:
                named = jnp.where(hit, (ref[1:2, here] + 1).astype(F32), 0.0)
                place = lax.broadcasted_iota(jnp.int32, (2 * CAP, part), 0) == rank + side * CAP
                place = jnp.where(place, 1.0, 0.0).astype(BF16)
                table = table + dot_nt(named.astype(BF16), place)
    table_ref[...] = table
    joined, first = jnp.full((1, rows), -1, jnp.int32), 0
    for row, chunk in ((1, NEAR), (8, MID), (6, NEAR), (5, MID)):
        local = slot_ref[row : row + 1, :]
        joined = jnp.where(local >= 0, local + first, joined)
        first += NX * len(chunk) * CAP
    for row in range(JOINED, slot_ref.shape[0]):
        slot_ref[row : row + 1, :] = joined


def message_body(feat_ref, w_ref, message_ref, *slope_ref):
    pre = dot(feat_ref[...], w_ref[...])
    sig = sigmoid(pre)
    message_ref[...] = (pre * sig).astype(BF16)
    if slope_ref:
        slope_ref[0][...] = (sig * (1.0 + pre * (1.0 - sig))).astype(BF16)


def message_of(feat, w, count):
    rows, width = feat.shape
    step = 512
    block = pl.BlockSpec((step, width), lambda i: (i, 0))
    return call(
        message_body,
        [shape((rows, width))] * count,
        feat,
        w,
        flops=2 * rows * width * width,
        bytes_accessed=8 * rows * width,
        grid=(rows // step,),
        in_specs=[block, pl.BlockSpec((width, width), lambda i: (0, 0))],
        out_specs=[block] * count,
    )


def route_body(chunk, slot_ref, own_ref, other_ref, *rest):
    outs = rest[-NX:]
    rows = slot_ref.shape[1]
    each = len(chunk) * CAP
    for side, ref in enumerate((own_ref, other_ref)):
        row = 2 * side + (0 if chunk == OUTER else 1)
        slot = slot_ref[row : row + 1, :]
        for xr in range(NX):
            place = lax.broadcasted_iota(jnp.int32, (each, rows), 0) + xr * each
            hits = jnp.where(place == slot, 1.0, 0.0).astype(BF16)
            outs[xr][pl.ds(side * each, each), :] = dot(hits, ref[...]).astype(BF16)
    if chunk == OUTER:
        for xr in range(NX):
            named = rest[0][pl.ds(xr * NZ, NZ), :]
            named = jnp.concatenate([named, jnp.zeros((NZ, 2 * CAP), F32)], axis=0)
            spare = outs[xr].shape[1] // (2 * CAP) - 1
            named = jnp.concatenate([named] + [jnp.zeros_like(named)] * spare, axis=1)
            outs[xr][pl.ds(2 * each, 2 * NZ), :] = named.astype(BF16)


def route(chunk, slot, own, other, *table, after=()):
    rows, width = own.shape
    return call(
        functools.partial(route_body, chunk),
        [shape((2 * len(chunk) * CAP + 2 * NZ * len(table), width))] * NX,
        slot,
        own,
        other,
        *table,
        after=after,
        flops=4 * NX * len(chunk) * CAP * rows * width,
        bytes_accessed=8 * rows * width,
    )


def by_distance(table_ref, k, blocks, at, each, nodes):
    node = (lax.broadcasted_iota(jnp.int32, (nodes, 2 * CAP), 0) + 1).astype(F32)
    total = None
    for xr in range(NX):
        hit = node == table_ref[xr * NZ + k : xr * NZ + k + 1, :]
        hits = jnp.where(hit, 1.0, 0.0).astype(BF16)
        held = [blocks[xr][pl.ds(side * each + at * CAP, CAP), :] for side in range(2)]
        term = dot(hits, jnp.concatenate(held, axis=0))
        total = term if total is None else total + term
    return total


def merge_outer_body(*refs):
    blocks, outs, (table_ref, turned_ref) = refs[:NX], refs[NX:-2], refs[-2:]
    each = len(OUTER) * CAP
    for xr in range(NX):
        named = blocks[xr][pl.ds(2 * each, 2 * NZ), :]
        table_ref[pl.ds(xr * NZ, NZ), :] = named[:NZ, : 2 * CAP].astype(F32)
    square = jnp.concatenate(
        [table_ref[...], jnp.zeros((2 * CAP - NX * NZ, 2 * CAP), F32)], axis=0
    )
    turned_ref[...] = square.T
    for at, k in enumerate(OUTER):
        total = by_distance(table_ref, k, blocks, at, each, outs[at].shape[0])
        outs[at][...] = total.astype(BF16)


def merge_near_body(table_ref, two, six, *refs):
    blocks, outs = refs[:NX], refs[NX:]
    relayed = {1: two, 7: six}
    for at, k in enumerate(NEAR):
        total = by_distance(table_ref, k, blocks, at, len(NEAR) * CAP, outs[at].shape[0])
        if k in relayed:
            total = total + relayed[k][...].astype(F32)
        outs[at][...] = total.astype(BF16)


def merge(chunk, blocks, nodes, *given, after=()):
    width = blocks[0].shape[1]
    outs = [shape((nodes, width))] * len(chunk)
    if chunk == OUTER:
        outs += [shape((NX * NZ, 2 * CAP), F32), shape((2 * CAP, 2 * CAP), F32)]
    return call(
        merge_outer_body if chunk == OUTER else merge_near_body,
        outs,
        *given,
        *blocks,
        after=after,
        flops=2 * len(chunk) * NX * nodes * 2 * CAP * width,
        bytes_accessed=6 * 1024 * width,
    )


def add_body(one, two, out):
    out[...] = (one[...].astype(F32) + two[...].astype(F32)).astype(BF16)


def add(one, two):
    return call(add_body, shape(one.shape), one, two)


def mesh_body(
    near, up, down, feat, cotangent, d_sender, w_mesh, w_edge, latent_ref, sender_ref,
    grad_ref, out
):
    total = near[...].astype(F32) + up[...].astype(F32) + down[...].astype(F32)
    pre_mesh = dot(total.astype(BF16), w_mesh[...])
    sig = sigmoid(pre_mesh)
    latent = (feat[...].astype(F32) + pre_mesh * sig).astype(BF16)
    latent_ref[...] = latent
    pre_edge = dot(latent, w_edge[...])
    edge_sig = sigmoid(pre_edge)
    sender_ref[...] = (pre_edge * edge_sig).astype(BF16)
    d_pre_edge = (d_sender[...] * (edge_sig * (1.0 + pre_edge * (1.0 - edge_sig)))).astype(BF16)
    d_latent = cotangent[...].astype(F32) + dot_nt(d_pre_edge, w_edge[...])
    grad_ref[...] = d_latent.astype(BF16)
    d_pre_mesh = (d_latent * (sig * (1.0 + pre_mesh * (1.0 - sig)))).astype(BF16)
    out[...] = dot_nt(d_pre_mesh, w_mesh[...]).astype(BF16)


def expand_body(chunk, turned, *refs):
    count = len(chunk)
    held, outs = refs[:count], refs[-NX:]
    for at, k in enumerate(chunk):
        values = held[at][...]
        node = (lax.broadcasted_iota(jnp.int32, (2 * CAP, values.shape[0]), 1) + 1).astype(F32)
        hits = []
        for xr in range(NX):
            hit = node == turned[:, xr * NZ + k : xr * NZ + k + 1]
            hits.append(jnp.where(hit, 1.0, 0.0).astype(BF16))
        moved = dot(jnp.concatenate(hits, axis=0), values).astype(BF16)
        for xr in range(NX):
            for side in range(2):
                first = (2 * xr + side) * CAP
                outs[xr][pl.ds((side * count + at) * CAP, CAP), :] = moved[first : first + CAP]


def expand(chunk, turned, held, after=()):
    width = held[0].shape[1]
    count = len(chunk)
    return call(
        functools.partial(expand_body, chunk),
        [shape((2 * count * CAP, width))] * NX,
        turned,
        *[held[k] for k in chunk],
        after=after,
        flops=2 * count * NX * 256 * 2 * CAP * width,
        bytes_accessed=6 * 1024 * width,
    )


def halves_body(*refs):
    blocks, out = refs[:-1], refs[-1]
    first = 0
    for ref in blocks:
        out[pl.ds(first, ref.shape[0]), :] = ref[...]
        first += ref.shape[0]


def halves(blocks, after):
    width = blocks[0].shape[1]
    sizes = [block.shape[0] // 2 for block in blocks]
    return call(
        halves_body,
        shape((sum(sizes), width)),
        *blocks,
        after=after,
        grid=(1,),
        in_specs=[pl.BlockSpec((size, width), lambda i: (1, 0)) for size in sizes],
        out_specs=pl.BlockSpec((sum(sizes), width), lambda i: (0, 0)),
        bytes_accessed=4 * sum(sizes) * width,
    )


def collect_body(column, count, adds, ends, *refs):
    slot_ref, held = refs[0], refs[-1]
    out = refs[-2]
    used = 2 if adds else 1
    blocks = refs[used : used + count]

    @pl.when(pl.program_id(0) == 0)
    def _():
        first = 0
        for ref in blocks:
            held[pl.ds(first, ref.shape[0]), :] = ref[...]
            first += ref.shape[0]

    slot = slot_ref[:, column : column + 1]
    place = lax.broadcasted_iota(jnp.int32, (slot.shape[0], held.shape[0]), 1)
    total = dot(jnp.where(place == slot, 1.0, 0.0).astype(BF16), held[...])
    if adds:
        total = total + refs[1][...].astype(F32)
    if ends:
        slope, w = refs[used + count], refs[used + count + 1]
        d_pre = (total * slope[...].astype(F32)).astype(BF16)
        out[...] = dot_nt(d_pre, w[...]).astype(BF16)
    else:
        out[...] = total.astype(BF16)


def collect(column, blocks, whole, slot_column, before=None, ends=()):
    blocks = list(blocks) + list(whole)
    rows, width = slot_column.shape[0], blocks[0].shape[1]
    step = 512
    part = pl.BlockSpec((step, width), lambda i: (i, 0))
    halved = len(blocks) - len(whole)
    sizes = [block.shape[0] // (2 if at < halved else 1) for at, block in enumerate(blocks)]
    prior = [] if before is None else [before]
    return call(
        functools.partial(collect_body, column, len(blocks), before is not None, bool(ends)),
        shape((rows, width)),
        slot_column,
        *prior,
        *blocks,
        *ends,
        grid=(rows // step,),
        in_specs=[pl.BlockSpec((step, slot_column.shape[1]), lambda i: (i, 0))]
        + [part] * len(prior)
        + [pl.BlockSpec((size, width), lambda i: (0, 0)) for size in sizes]
        + ([part, pl.BlockSpec((width, width), lambda i: (0, 0))] if ends else []),
        out_specs=part,
        scratch_shapes=[pltpu.VMEM((sum(sizes), width), BF16)],
        flops=2 * rows * sum(sizes) * width,
        bytes_accessed=4 * rows * width,
    )


def band_of(z, x, core):
    return (z % NZ) * 2 * NX + (x % NX) * 2 + core


def shift(value, dz=0, dx=0, dcore=0):
    pairs = [
        (band_of(z, x, core), band_of(z + dz, x + dx, core ^ dcore))
        for z in range(NZ)
        for x in range(NX)
        for core in range(2)
    ]
    return lax.ppermute(value, "band", pairs)


def along_patch(value, by):
    size = lax.axis_size("patch")
    return lax.ppermute(value, "patch", [(i, (i + by) % size) for i in range(size)])


def local(
    grid_feat, mesh_feat, grid_band, grid_target, mesh_nbr, w_in, w_mesh, w_edge, w_out, cotangent
):
    mesh_rows, width = mesh_feat.shape
    rows = grid_feat.shape[0]
    band = lax.axis_index("band")
    here = jnp.stack([band // (2 * NX), (band // 2) % NX, band % 2])
    named = jnp.stack([grid_band[:, 0], grid_target])
    other_named = shift(named, dcore=1)
    other_feat = shift(grid_feat, dcore=1)
    inside = pl.BlockSpec(memory_space=pltpu.VMEM)
    slot, table = call(
        index_body,
        [shape((16, rows), jnp.int32), shape((NX * NZ, 2 * CAP), F32)],
        here,
        named,
        other_named,
        in_specs=[pl.BlockSpec(memory_space=pltpu.SMEM), inside, inside],
    )
    slot_column = slot.T
    own, slope = message_of(grid_feat, w_in, 2)
    (other,) = message_of(other_feat, w_in, 1)

    span = jnp.arange(mesh_rows + 2 * HALO, dtype=jnp.int32)
    adjacency = jnp.zeros((mesh_rows, mesh_rows + 2 * HALO), F32)
    for column in range(mesh_nbr.shape[1]):
        adjacency = adjacency + (mesh_nbr[:, column : column + 1] == span[None, :]).astype(F32)
    adjacency = adjacency.astype(BF16)
    d_edge = dot(cotangent, w_out.T).astype(BF16)
    d_extended = lax.dot_general(
        adjacency, d_edge, (((0,), (0,)), ((), ())), preferred_element_type=F32
    )
    from_next = along_patch(d_extended[:HALO].astype(BF16), -1).astype(F32)
    from_prev = along_patch(d_extended[HALO + mesh_rows :].astype(BF16), 1).astype(F32)
    d_sender = d_extended[HALO : HALO + mesh_rows]
    d_sender = d_sender.at[:HALO].add(from_prev).at[mesh_rows - HALO :].add(from_next)

    def along_x(sent, way):
        return [sent[0]] + [shift(sent[k], dx=way * k) for k in range(1, NX)]

    sent = route(OUTER, slot, own, other, table)
    arrived = along_x(sent, 1)
    sent_near = route(NEAR, slot, own, other, after=(slot_column,))
    arrived_near = along_x(sent_near, 1)
    three, four, five, two, six, listed, turned = merge(
        OUTER, arrived, mesh_rows, after=(sent_near[1],)
    )
    four, five = shift(four, dz=1), shift(five, dz=-1)
    three = shift(add(three, four), dz=1)
    two, six = shift(add(two, three), dz=1), shift(add(six, five), dz=-1)
    up, down, near = merge(NEAR, arrived_near, mesh_rows, listed, two, six)
    up, down = shift(up, dz=1), shift(down, dz=-1)

    node = shape((mesh_rows, width))
    latent, sender, mesh_grad, mine = call(
        mesh_body,
        [node, node, node, node],
        near,
        up,
        down,
        mesh_feat,
        cotangent,
        d_sender,
        w_mesh,
        w_edge,
        flops=8 * mesh_rows * width * width,
        bytes_accessed=20 * mesh_rows * width,
    )

    before = along_patch(sender[mesh_rows - HALO :], 1)
    after = along_patch(sender[:HALO], -1)
    extended = jnp.concatenate([before, sender, after], axis=0)
    edge_total = dot(adjacency, extended).astype(BF16)
    mesh_out = (latent.astype(F32) + dot(edge_total, w_out)).astype(BF16)

    held = [mine] * NZ
    for k in range(1, NZ // 2 + 1):
        held[k] = shift(held[k - 1], dz=-1)
    for k in range(NZ - 1, NZ // 2, -1):
        held[k] = shift(held[(k + 1) % NZ], dz=1)
    arrived = along_x(expand(NEAR, turned, held, (mesh_out,)), -1)
    arrived += along_x(expand(MID, turned, held), -1)
    sent = expand(FAR, turned, held)
    swapped = shift(halves(arrived, (sent[0],)), dcore=1)
    total = collect(JOINED, arrived, (swapped,), slot_column)
    arrived = along_x(sent, -1)
    swapped = shift(halves(arrived, (total,)), dcore=1)
    total = collect(7, arrived, (), slot_column, total)
    grid_grad = collect(4, (), (swapped,), slot_column, total, (slope, w_in))
    return mesh_out, mesh_grad, grid_grad


def solution(mesh):
    spread = P(("band", "patch"), None)
    return jax.shard_map(
        local,
        mesh=mesh,
        in_specs=(
            spread,
            spread,
            spread,
            P(("band", "patch")),
            spread,
            P(),
            P(),
            P(),
            P(),
            spread,
        ),
        out_specs=(spread, spread, spread),
        check_vma=False,
    )
```

```python
import functools

import jax
import jax.numpy as jnp
from jax import lax
from jax.experimental import pallas as pl
from jax.experimental.pallas import tpu as pltpu
from jax.sharding import PartitionSpec as P

HALO = 64
NZ = 8
NX = 4
CAP = 64
FAR, MID, NEAR = (3, 4, 5), (2, 6), (1, 7, 0)
PARTS = (FAR, MID, NEAR)
JOINED = 9
VMEM = 36 * 2**20
F32 = jnp.float32
BF16 = jnp.bfloat16


def sigmoid(v):
    return 0.5 * jnp.tanh(0.5 * v) + 0.5


def call(body, outs, *args, after=(), flops=0, bytes_accessed=0, **kw):
    if after:
        inner, count, extra = body, len(args), len(after)
        kw["in_specs"] = list(kw.get("in_specs") or [pl.BlockSpec(memory_space=pltpu.VMEM)] * count)
        kw["in_specs"] += [pl.BlockSpec(memory_space=pl.ANY)] * extra

        def body(*refs):
            inner(*refs[:count], *refs[count + extra :])

    return pl.pallas_call(
        body,
        out_shape=outs,
        compiler_params=pltpu.CompilerParams(vmem_limit_bytes=VMEM),
        cost_estimate=pl.CostEstimate(flops=0, bytes_accessed=0, transcendentals=0),
        **kw,
    )(*args, *after)


def shape(dims, dtype=BF16):
    return jax.ShapeDtypeStruct(dims, dtype)


def dot(a, b):
    return jnp.dot(a, b, preferred_element_type=F32)


def dot_nt(a, b):
    return lax.dot_general(a, b, (((1,), (1,)), ((), ())), preferred_element_type=F32)


def index_body(here_ref, own_ref, other_ref, slot_ref, table_ref):
    rows = own_ref.shape[1]
    part = 256
    below = lax.broadcasted_iota(jnp.int32, (part, part), 0)
    upper = jnp.where(below <= lax.broadcasted_iota(jnp.int32, (part, part), 1), 1.0, 0.0)
    upper = upper.astype(BF16)
    here_z, here_x, here_core = here_ref[0], here_ref[1], here_ref[2]
    table = jnp.zeros((NX * NZ, 2 * CAP), F32)
    for side, ref in enumerate((own_ref, other_ref, own_ref)):
        carry = jnp.zeros((NX * NZ, 1), F32)
        wanted = here_core if side < 2 else 1 - here_core
        for first in range(0, rows, part):
            here = pl.ds(first, part)
            band = ref[0:1, here]
            k = ((band >> 3) - here_z) & (NZ - 1)
            xr = ((band >> 1) - here_x) & (NX - 1)
            kept = (band & 1) == wanted
            q = jnp.where(kept, xr * NZ + k, -1)
            hit = lax.broadcasted_iota(jnp.int32, (NX * NZ, part), 0) == q
            hits = jnp.where(hit, 1.0, 0.0)
            counted = dot(hits.astype(BF16), upper) + carry
            rank = jnp.sum(hits * counted, axis=0, keepdims=True) - 1.0
            carry = counted[:, part - 1 : part]
            rank = rank.astype(jnp.int32)
            for row, chunk in enumerate(PARTS, 3 * side):
                at = jnp.full_like(q, -1)
                for place, distance in enumerate(chunk):
                    at = jnp.where(k == distance, place, at)
                local = (xr * len(chunk) + at) * CAP + rank
                slot_ref[row : row + 1, here] = jnp.where(kept & (at >= 0), local, -1)
            if side < 2:
                named = jnp.where(hit, (ref[1:2, here] + 1).astype(F32), 0.0)
                place = lax.broadcasted_iota(jnp.int32, (2 * CAP, part), 0) == rank + side * CAP
                place = jnp.where(place, 1.0, 0.0).astype(BF16)
                table = table + dot_nt(named.astype(BF16), place)
    table_ref[...] = table
    joined, first = jnp.full((1, rows), -1, jnp.int32), 0
    for row, chunk in ((2, NEAR), (1, MID), (8, NEAR), (7, MID)):
        local = slot_ref[row : row + 1, :]
        joined = jnp.where(local >= 0, local + first, joined)
        first += NX * len(chunk) * CAP
    for row in range(JOINED, slot_ref.shape[0]):
        slot_ref[row : row + 1, :] = joined


def message_body(feat_ref, w_ref, message_ref, *slope_ref):
    pre = dot(feat_ref[...], w_ref[...])
    sig = sigmoid(pre)
    message_ref[...] = (pre * sig).astype(BF16)
    if slope_ref:
        slope_ref[0][...] = (sig * (1.0 + pre * (1.0 - sig))).astype(BF16)


def message_of(feat, w, count):
    rows, width = feat.shape
    step = 512
    block = pl.BlockSpec((step, width), lambda i: (i, 0))
    return call(
        message_body,
        [shape((rows, width))] * count,
        feat,
        w,
        flops=2 * rows * width * width,
        bytes_accessed=8 * rows * width,
        grid=(rows // step,),
        in_specs=[block, pl.BlockSpec((width, width), lambda i: (0, 0))],
        out_specs=[block] * count,
    )


def route_body(chunk, slot_ref, own_ref, other_ref, *rest):
    outs = rest[-NX:]
    rows = slot_ref.shape[1]
    each = len(chunk) * CAP
    for side, ref in enumerate((own_ref, other_ref)):
        row = 3 * side + PARTS.index(chunk)
        slot = slot_ref[row : row + 1, :]
        for xr in range(NX):
            place = lax.broadcasted_iota(jnp.int32, (each, rows), 0) + xr * each
            hits = jnp.where(place == slot, 1.0, 0.0).astype(BF16)
            outs[xr][pl.ds(side * each, each), :] = dot(hits, ref[...]).astype(BF16)
    if chunk == FAR:
        for xr in range(NX):
            named = rest[0][pl.ds(xr * NZ, NZ), :]
            named = jnp.concatenate([named, jnp.zeros((NZ, 2 * CAP), F32)], axis=0)
            spare = outs[xr].shape[1] // (2 * CAP) - 1
            named = jnp.concatenate([named] + [jnp.zeros_like(named)] * spare, axis=1)
            outs[xr][pl.ds(2 * each, 2 * NZ), :] = named.astype(BF16)


def route(chunk, slot, own, other, *table, after=()):
    rows, width = own.shape
    return call(
        functools.partial(route_body, chunk),
        [shape((2 * len(chunk) * CAP + 2 * NZ * len(table), width))] * NX,
        slot,
        own,
        other,
        *table,
        after=after,
        flops=4 * NX * len(chunk) * CAP * rows * width,
        bytes_accessed=8 * rows * width,
    )


def by_distance(table_ref, k, blocks, at, each, nodes):
    node = (lax.broadcasted_iota(jnp.int32, (nodes, 2 * CAP), 0) + 1).astype(F32)
    total = None
    for xr in range(NX):
        hit = node == table_ref[xr * NZ + k : xr * NZ + k + 1, :]
        hits = jnp.where(hit, 1.0, 0.0).astype(BF16)
        held = [blocks[xr][pl.ds(side * each + at * CAP, CAP), :] for side in range(2)]
        term = dot(hits, jnp.concatenate(held, axis=0))
        total = term if total is None else total + term
    return total


def merge_far_body(*refs):
    blocks, outs, (table_ref, turned_ref) = refs[:NX], refs[NX:-2], refs[-2:]
    each = len(FAR) * CAP
    for xr in range(NX):
        named = blocks[xr][pl.ds(2 * each, 2 * NZ), :]
        table_ref[pl.ds(xr * NZ, NZ), :] = named[:NZ, : 2 * CAP].astype(F32)
    square = jnp.concatenate(
        [table_ref[...], jnp.zeros((2 * CAP - NX * NZ, 2 * CAP), F32)], axis=0
    )
    turned_ref[...] = square.T
    for at, k in enumerate(FAR):
        total = by_distance(table_ref, k, blocks, at, each, outs[at].shape[0])
        outs[at][...] = total.astype(BF16)


def merge_body(chunk, table_ref, above, below, *refs):
    blocks, outs = refs[:NX], refs[NX:]
    relayed = {chunk[0]: above, chunk[1]: below}
    for at, k in enumerate(chunk):
        total = by_distance(table_ref, k, blocks, at, len(chunk) * CAP, outs[at].shape[0])
        if k in relayed:
            total = total + relayed[k][...].astype(F32)
        outs[at][...] = total.astype(BF16)


def merge(chunk, blocks, nodes, *given, after=()):
    width = blocks[0].shape[1]
    outs = [shape((nodes, width))] * len(chunk)
    if chunk == FAR:
        outs += [shape((NX * NZ, 2 * CAP), F32), shape((2 * CAP, 2 * CAP), F32)]
    return call(
        merge_far_body if chunk == FAR else functools.partial(merge_body, chunk),
        outs,
        *given,
        *blocks,
        after=after,
        flops=2 * len(chunk) * NX * nodes * 2 * CAP * width,
        bytes_accessed=6 * 1024 * width,
    )


def add_body(one, two, out):
    out[...] = (one[...].astype(F32) + two[...].astype(F32)).astype(BF16)


def add(one, two):
    return call(add_body, shape(one.shape), one, two)


def mesh_body(
    near, up, down, feat, cotangent, d_sender, w_mesh, w_edge, latent_ref, sender_ref,
    grad_ref, out
):
    total = near[...].astype(F32) + up[...].astype(F32) + down[...].astype(F32)
    pre_mesh = dot(total.astype(BF16), w_mesh[...])
    sig = sigmoid(pre_mesh)
    latent = (feat[...].astype(F32) + pre_mesh * sig).astype(BF16)
    latent_ref[...] = latent
    pre_edge = dot(latent, w_edge[...])
    edge_sig = sigmoid(pre_edge)
    sender_ref[...] = (pre_edge * edge_sig).astype(BF16)
    d_pre_edge = (d_sender[...] * (edge_sig * (1.0 + pre_edge * (1.0 - edge_sig)))).astype(BF16)
    d_latent = cotangent[...].astype(F32) + dot_nt(d_pre_edge, w_edge[...])
    grad_ref[...] = d_latent.astype(BF16)
    d_pre_mesh = (d_latent * (sig * (1.0 + pre_mesh * (1.0 - sig)))).astype(BF16)
    out[...] = dot_nt(d_pre_mesh, w_mesh[...]).astype(BF16)


def expand_body(chunk, turned, *refs):
    count = len(chunk)
    held, outs = refs[:count], refs[-NX:]
    for at, k in enumerate(chunk):
        values = held[at][...]
        node = (lax.broadcasted_iota(jnp.int32, (2 * CAP, values.shape[0]), 1) + 1).astype(F32)
        hits = []
        for xr in range(NX):
            hit = node == turned[:, xr * NZ + k : xr * NZ + k + 1]
            hits.append(jnp.where(hit, 1.0, 0.0).astype(BF16))
        moved = dot(jnp.concatenate(hits, axis=0), values).astype(BF16)
        for xr in range(NX):
            for side in range(2):
                first = (2 * xr + side) * CAP
                outs[xr][pl.ds((side * count + at) * CAP, CAP), :] = moved[first : first + CAP]


def expand(chunk, turned, held, after=()):
    width = held[0].shape[1]
    count = len(chunk)
    return call(
        functools.partial(expand_body, chunk),
        [shape((2 * count * CAP, width))] * NX,
        turned,
        *[held[k] for k in chunk],
        after=after,
        flops=2 * count * NX * 256 * 2 * CAP * width,
        bytes_accessed=6 * 1024 * width,
    )


def halves_body(*refs):
    blocks, out = refs[:-1], refs[-1]
    first = 0
    for ref in blocks:
        out[pl.ds(first, ref.shape[0]), :] = ref[...]
        first += ref.shape[0]


def halves(blocks, after):
    width = blocks[0].shape[1]
    sizes = [block.shape[0] // 2 for block in blocks]
    return call(
        halves_body,
        shape((sum(sizes), width)),
        *blocks,
        after=after,
        grid=(1,),
        in_specs=[pl.BlockSpec((size, width), lambda i: (1, 0)) for size in sizes],
        out_specs=pl.BlockSpec((sum(sizes), width), lambda i: (0, 0)),
        bytes_accessed=4 * sum(sizes) * width,
    )


def collect_body(column, count, adds, ends, *refs):
    slot_ref, held = refs[0], refs[-1]
    out = refs[-2]
    used = 2 if adds else 1
    blocks = refs[used : used + count]

    @pl.when(pl.program_id(0) == 0)
    def _():
        first = 0
        for ref in blocks:
            held[pl.ds(first, ref.shape[0]), :] = ref[...]
            first += ref.shape[0]

    slot = slot_ref[:, column : column + 1]
    place = lax.broadcasted_iota(jnp.int32, (slot.shape[0], held.shape[0]), 1)
    total = dot(jnp.where(place == slot, 1.0, 0.0).astype(BF16), held[...])
    if adds:
        total = total + refs[1][...].astype(F32)
    if ends:
        slope, w = refs[used + count], refs[used + count + 1]
        d_pre = (total * slope[...].astype(F32)).astype(BF16)
        out[...] = dot_nt(d_pre, w[...]).astype(BF16)
    else:
        out[...] = total.astype(BF16)


def collect(column, blocks, whole, slot_column, before=None, ends=()):
    blocks = list(blocks) + list(whole)
    rows, width = slot_column.shape[0], blocks[0].shape[1]
    step = 512
    part = pl.BlockSpec((step, width), lambda i: (i, 0))
    halved = len(blocks) - len(whole)
    sizes = [block.shape[0] // (2 if at < halved else 1) for at, block in enumerate(blocks)]
    prior = [] if before is None else [before]
    return call(
        functools.partial(collect_body, column, len(blocks), before is not None, bool(ends)),
        shape((rows, width)),
        slot_column,
        *prior,
        *blocks,
        *ends,
        grid=(rows // step,),
        in_specs=[pl.BlockSpec((step, slot_column.shape[1]), lambda i: (i, 0))]
        + [part] * len(prior)
        + [pl.BlockSpec((size, width), lambda i: (0, 0)) for size in sizes]
        + ([part, pl.BlockSpec((width, width), lambda i: (0, 0))] if ends else []),
        out_specs=part,
        scratch_shapes=[pltpu.VMEM((sum(sizes), width), BF16)],
        flops=2 * rows * sum(sizes) * width,
        bytes_accessed=4 * rows * width,
    )


def band_of(z, x, core):
    return (z % NZ) * 2 * NX + (x % NX) * 2 + core


def shift(value, dz=0, dx=0, dcore=0):
    pairs = [
        (band_of(z, x, core), band_of(z + dz, x + dx, core ^ dcore))
        for z in range(NZ)
        for x in range(NX)
        for core in range(2)
    ]
    return lax.ppermute(value, "band", pairs)


def along_patch(value, by):
    size = lax.axis_size("patch")
    return lax.ppermute(value, "patch", [(i, (i + by) % size) for i in range(size)])


def local(
    grid_feat, mesh_feat, grid_band, grid_target, mesh_nbr, w_in, w_mesh, w_edge, w_out, cotangent
):
    mesh_rows, width = mesh_feat.shape
    rows = grid_feat.shape[0]
    band = lax.axis_index("band")
    here = jnp.stack([band // (2 * NX), (band // 2) % NX, band % 2])
    named = jnp.stack([grid_band[:, 0], grid_target])
    other_named = shift(named, dcore=1)
    other_feat = shift(grid_feat, dcore=1)
    inside = pl.BlockSpec(memory_space=pltpu.VMEM)
    slot, table = call(
        index_body,
        [shape((16, rows), jnp.int32), shape((NX * NZ, 2 * CAP), F32)],
        here,
        named,
        other_named,
        in_specs=[pl.BlockSpec(memory_space=pltpu.SMEM), inside, inside],
    )
    slot_column = slot.T
    own, slope = message_of(grid_feat, w_in, 2)
    (other,) = message_of(other_feat, w_in, 1)

    span = jnp.arange(mesh_rows + 2 * HALO, dtype=jnp.int32)
    adjacency = jnp.zeros((mesh_rows, mesh_rows + 2 * HALO), F32)
    for column in range(mesh_nbr.shape[1]):
        adjacency = adjacency + (mesh_nbr[:, column : column + 1] == span[None, :]).astype(F32)
    adjacency = adjacency.astype(BF16)
    d_edge = dot(cotangent, w_out.T).astype(BF16)
    d_extended = lax.dot_general(
        adjacency, d_edge, (((0,), (0,)), ((), ())), preferred_element_type=F32
    )
    from_next = along_patch(d_extended[:HALO].astype(BF16), -1).astype(F32)
    from_prev = along_patch(d_extended[HALO + mesh_rows :].astype(BF16), 1).astype(F32)
    d_sender = d_extended[HALO : HALO + mesh_rows]
    d_sender = d_sender.at[:HALO].add(from_prev).at[mesh_rows - HALO :].add(from_next)

    def along_x(sent, way):
        return [sent[0]] + [shift(sent[k], dx=way * k) for k in range(1, NX)]

    sent = route(FAR, slot, own, other, table)
    arrived = along_x(sent, 1)
    sent_mid = route(MID, slot, own, other, after=(slot_column,))
    arrived_mid = along_x(sent_mid, 1)
    sent_near = route(NEAR, slot, own, other, after=(sent_mid[1],))
    arrived_near = along_x(sent_near, 1)
    three, four, five, listed, turned = merge(FAR, arrived, mesh_rows, after=(sent_near[1], d_extended))
    four, five = shift(four, dz=1), shift(five, dz=-1)
    three = shift(add(three, four), dz=1)
    two, six = merge(MID, arrived_mid, mesh_rows, listed, three, five)
    two, six = shift(two, dz=1), shift(six, dz=-1)
    up, down, near = merge(NEAR, arrived_near, mesh_rows, listed, two, six)
    up, down = shift(up, dz=1), shift(down, dz=-1)

    node = shape((mesh_rows, width))
    latent, sender, mesh_grad, mine = call(
        mesh_body,
        [node, node, node, node],
        near,
        up,
        down,
        mesh_feat,
        cotangent,
        d_sender,
        w_mesh,
        w_edge,
        flops=8 * mesh_rows * width * width,
        bytes_accessed=20 * mesh_rows * width,
    )

    before = along_patch(sender[mesh_rows - HALO :], 1)
    after = along_patch(sender[:HALO], -1)
    extended = jnp.concatenate([before, sender, after], axis=0)
    edge_total = dot(adjacency, extended).astype(BF16)
    mesh_out = (latent.astype(F32) + dot(edge_total, w_out)).astype(BF16)

    held = [mine] * NZ
    for k in range(1, NZ // 2 + 1):
        held[k] = shift(held[k - 1], dz=-1)
    for k in range(NZ - 1, NZ // 2, -1):
        held[k] = shift(held[(k + 1) % NZ], dz=1)
    arrived = along_x(expand(NEAR, turned, held, (mesh_out,)), -1)
    arrived += along_x(expand(MID, turned, held), -1)
    sent = expand(FAR, turned, held)
    swapped = shift(halves(arrived, (sent[0],)), dcore=1)
    total = collect(JOINED, arrived, (swapped,), slot_column)
    arrived = along_x(sent, -1)
    swapped = shift(halves(arrived, (total,)), dcore=1)
    total = collect(0, arrived, (), slot_column, total)
    grid_grad = collect(6, (), (swapped,), slot_column, total, (slope, w_in))
    return mesh_out, mesh_grad, grid_grad


def solution(mesh):
    spread = P(("band", "patch"), None)
    return jax.shard_map(
        local,
        mesh=mesh,
        in_specs=(
            spread,
            spread,
            spread,
            P(("band", "patch")),
            spread,
            P(),
            P(),
            P(),
            P(),
            spread,
        ),
        out_specs=(spread, spread, spread),
        check_vma=False,
    )
```

```python
import functools

import jax
import jax.numpy as jnp
from jax import lax
from jax.experimental import pallas as pl
from jax.experimental.pallas import tpu as pltpu
from jax.sharding import PartitionSpec as P

HALO = 64
NZ = 8
NX = 4
CAP = 64
FAR, MID, NEAR = (3, 4, 5), (2, 6), (1, 7, 0)
PARTS = (FAR, MID, NEAR)
JOINED = 9
VMEM = 36 * 2**20
F32 = jnp.float32
BF16 = jnp.bfloat16


def sigmoid(v):
    return 0.5 * jnp.tanh(0.5 * v) + 0.5


def call(body, outs, *args, after=(), vmem=VMEM, flops=0, bytes_accessed=0, **kw):
    if after:
        inner, count, extra = body, len(args), len(after)
        kw["in_specs"] = list(kw.get("in_specs") or [pl.BlockSpec(memory_space=pltpu.VMEM)] * count)
        kw["in_specs"] += [pl.BlockSpec(memory_space=pl.ANY)] * extra

        def body(*refs):
            inner(*refs[:count], *refs[count + extra :])

    return pl.pallas_call(
        body,
        out_shape=outs,
        compiler_params=pltpu.CompilerParams(vmem_limit_bytes=vmem),
        cost_estimate=pl.CostEstimate(flops=0, bytes_accessed=0, transcendentals=0),
        **kw,
    )(*args, *after)


def shape(dims, dtype=BF16):
    return jax.ShapeDtypeStruct(dims, dtype)


def dot(a, b):
    return jnp.dot(a, b, preferred_element_type=F32)


def dot_nt(a, b):
    return lax.dot_general(a, b, (((1,), (1,)), ((), ())), preferred_element_type=F32)


def index_body(here_ref, own_ref, other_ref, slot_ref, table_ref):
    rows = own_ref.shape[1]
    part = 256
    below = lax.broadcasted_iota(jnp.int32, (part, part), 0)
    upper = jnp.where(below <= lax.broadcasted_iota(jnp.int32, (part, part), 1), 1.0, 0.0)
    upper = upper.astype(BF16)
    here_z, here_x, here_core = here_ref[0], here_ref[1], here_ref[2]
    table = jnp.zeros((NX * NZ, 2 * CAP), F32)
    for side, ref in enumerate((own_ref, other_ref, own_ref)):
        carry = jnp.zeros((NX * NZ, 1), F32)
        wanted = here_core if side < 2 else 1 - here_core
        for first in range(0, rows, part):
            here = pl.ds(first, part)
            band = ref[0:1, here]
            k = ((band >> 3) - here_z) & (NZ - 1)
            xr = ((band >> 1) - here_x) & (NX - 1)
            kept = (band & 1) == wanted
            q = jnp.where(kept, xr * NZ + k, -1)
            hit = lax.broadcasted_iota(jnp.int32, (NX * NZ, part), 0) == q
            hits = jnp.where(hit, 1.0, 0.0)
            counted = dot(hits.astype(BF16), upper) + carry
            rank = jnp.sum(hits * counted, axis=0, keepdims=True) - 1.0
            carry = counted[:, part - 1 : part]
            rank = rank.astype(jnp.int32)
            for row, chunk in enumerate(PARTS, 3 * side):
                at = jnp.full_like(q, -1)
                for place, distance in enumerate(chunk):
                    at = jnp.where(k == distance, place, at)
                local = (xr * len(chunk) + at) * CAP + rank
                slot_ref[row : row + 1, here] = jnp.where(kept & (at >= 0), local, -1)
            if side < 2:
                named = jnp.where(hit, (ref[1:2, here] + 1).astype(F32), 0.0)
                place = lax.broadcasted_iota(jnp.int32, (2 * CAP, part), 0) == rank + side * CAP
                place = jnp.where(place, 1.0, 0.0).astype(BF16)
                table = table + dot_nt(named.astype(BF16), place)
    table_ref[...] = table
    joined, first = jnp.full((1, rows), -1, jnp.int32), 0
    for row, chunk in ((2, NEAR), (1, MID), (8, NEAR), (7, MID)):
        local = slot_ref[row : row + 1, :]
        joined = jnp.where(local >= 0, local + first, joined)
        first += NX * len(chunk) * CAP
    for row in range(JOINED, slot_ref.shape[0]):
        slot_ref[row : row + 1, :] = joined


def message_body(feat_ref, w_ref, message_ref, *slope_ref):
    pre = dot(feat_ref[...], w_ref[...])
    sig = sigmoid(pre)
    message_ref[...] = (pre * sig).astype(BF16)
    if slope_ref:
        slope_ref[0][...] = (sig * (1.0 + pre * (1.0 - sig))).astype(BF16)


def message_of(feat, w, count):
    rows, width = feat.shape
    step = 512
    block = pl.BlockSpec((step, width), lambda i: (i, 0))
    return call(
        message_body,
        [shape((rows, width))] * count,
        feat,
        w,
        vmem=58 * 2**20 if count > 1 else VMEM,
        flops=2 * rows * width * width,
        bytes_accessed=8 * rows * width,
        grid=(rows // step,),
        in_specs=[block, pl.BlockSpec((width, width), lambda i: (0, 0))],
        out_specs=[block] * count,
    )


def route_body(chunk, slot_ref, own_ref, other_ref, *rest):
    outs = rest[-NX:]
    rows = slot_ref.shape[1]
    each = len(chunk) * CAP
    for side, ref in enumerate((own_ref, other_ref)):
        row = 3 * side + PARTS.index(chunk)
        slot = slot_ref[row : row + 1, :]
        for xr in range(NX):
            place = lax.broadcasted_iota(jnp.int32, (each, rows), 0) + xr * each
            hits = jnp.where(place == slot, 1.0, 0.0).astype(BF16)
            outs[xr][pl.ds(side * each, each), :] = dot(hits, ref[...]).astype(BF16)
    if chunk == FAR:
        for xr in range(NX):
            named = rest[0][pl.ds(xr * NZ, NZ), :]
            named = jnp.concatenate([named, jnp.zeros((NZ, 2 * CAP), F32)], axis=0)
            spare = outs[xr].shape[1] // (2 * CAP) - 1
            named = jnp.concatenate([named] + [jnp.zeros_like(named)] * spare, axis=1)
            outs[xr][pl.ds(2 * each, 2 * NZ), :] = named.astype(BF16)


def route(chunk, slot, own, other, *table, after=()):
    rows, width = own.shape
    return call(
        functools.partial(route_body, chunk),
        [shape((2 * len(chunk) * CAP + 2 * NZ * len(table), width))] * NX,
        slot,
        own,
        other,
        *table,
        after=after,
        flops=4 * NX * len(chunk) * CAP * rows * width,
        bytes_accessed=8 * rows * width,
    )


def by_distance(table_ref, k, blocks, at, each, nodes):
    node = (lax.broadcasted_iota(jnp.int32, (nodes, 2 * CAP), 0) + 1).astype(F32)
    total = None
    for xr in range(NX):
        hit = node == table_ref[xr * NZ + k : xr * NZ + k + 1, :]
        hits = jnp.where(hit, 1.0, 0.0).astype(BF16)
        held = [blocks[xr][pl.ds(side * each + at * CAP, CAP), :] for side in range(2)]
        term = dot(hits, jnp.concatenate(held, axis=0))
        total = term if total is None else total + term
    return total


def merge_far_body(*refs):
    blocks, outs, (table_ref, turned_ref) = refs[:NX], refs[NX:-2], refs[-2:]
    each = len(FAR) * CAP
    for xr in range(NX):
        named = blocks[xr][pl.ds(2 * each, 2 * NZ), :]
        table_ref[pl.ds(xr * NZ, NZ), :] = named[:NZ, : 2 * CAP].astype(F32)
    square = jnp.concatenate(
        [table_ref[...], jnp.zeros((2 * CAP - NX * NZ, 2 * CAP), F32)], axis=0
    )
    turned_ref[...] = square.T
    for at, k in enumerate(FAR):
        total = by_distance(table_ref, k, blocks, at, each, outs[at].shape[0])
        outs[at][...] = total.astype(BF16)


def merge_body(chunk, table_ref, above, below, *refs):
    blocks, outs = refs[:NX], refs[NX:]
    relayed = {chunk[0]: above, chunk[1]: below}
    for at, k in enumerate(chunk):
        total = by_distance(table_ref, k, blocks, at, len(chunk) * CAP, outs[at].shape[0])
        if k in relayed:
            total = total + relayed[k][...].astype(F32)
        outs[at][...] = total.astype(BF16)


def merge(chunk, blocks, nodes, *given, after=()):
    width = blocks[0].shape[1]
    outs = [shape((nodes, width))] * len(chunk)
    if chunk == FAR:
        outs += [shape((NX * NZ, 2 * CAP), F32), shape((2 * CAP, 2 * CAP), F32)]
    return call(
        merge_far_body if chunk == FAR else functools.partial(merge_body, chunk),
        outs,
        *given,
        *blocks,
        after=after,
        flops=2 * len(chunk) * NX * nodes * 2 * CAP * width,
        bytes_accessed=6 * 1024 * width,
    )


def add_body(one, two, out):
    out[...] = (one[...].astype(F32) + two[...].astype(F32)).astype(BF16)


def add(one, two):
    return call(add_body, shape(one.shape), one, two)


def mesh_body(
    near, up, down, feat, cotangent, d_sender, w_mesh, w_edge, latent_ref, sender_ref,
    grad_ref, out
):
    total = near[...].astype(F32) + up[...].astype(F32) + down[...].astype(F32)
    pre_mesh = dot(total.astype(BF16), w_mesh[...])
    sig = sigmoid(pre_mesh)
    latent = (feat[...].astype(F32) + pre_mesh * sig).astype(BF16)
    latent_ref[...] = latent
    pre_edge = dot(latent, w_edge[...])
    edge_sig = sigmoid(pre_edge)
    sender_ref[...] = (pre_edge * edge_sig).astype(BF16)
    d_pre_edge = (d_sender[...] * (edge_sig * (1.0 + pre_edge * (1.0 - edge_sig)))).astype(BF16)
    d_latent = cotangent[...].astype(F32) + dot_nt(d_pre_edge, w_edge[...])
    grad_ref[...] = d_latent.astype(BF16)
    d_pre_mesh = (d_latent * (sig * (1.0 + pre_mesh * (1.0 - sig)))).astype(BF16)
    out[...] = dot_nt(d_pre_mesh, w_mesh[...]).astype(BF16)


def expand_body(chunk, turned, *refs):
    count = len(chunk)
    held, outs = refs[:count], refs[-NX:]
    for at, k in enumerate(chunk):
        values = held[at][...]
        node = (lax.broadcasted_iota(jnp.int32, (2 * CAP, values.shape[0]), 1) + 1).astype(F32)
        hits = []
        for xr in range(NX):
            hit = node == turned[:, xr * NZ + k : xr * NZ + k + 1]
            hits.append(jnp.where(hit, 1.0, 0.0).astype(BF16))
        moved = dot(jnp.concatenate(hits, axis=0), values).astype(BF16)
        for xr in range(NX):
            for side in range(2):
                first = (2 * xr + side) * CAP
                outs[xr][pl.ds((side * count + at) * CAP, CAP), :] = moved[first : first + CAP]


def expand(chunk, turned, held, after=()):
    width = held[0].shape[1]
    count = len(chunk)
    return call(
        functools.partial(expand_body, chunk),
        [shape((2 * count * CAP, width))] * NX,
        turned,
        *[held[k] for k in chunk],
        after=after,
        flops=2 * count * NX * 256 * 2 * CAP * width,
        bytes_accessed=6 * 1024 * width,
    )


def halves_body(*refs):
    blocks, out = refs[:-1], refs[-1]
    first = 0
    for ref in blocks:
        out[pl.ds(first, ref.shape[0]), :] = ref[...]
        first += ref.shape[0]


def halves(blocks, after):
    width = blocks[0].shape[1]
    sizes = [block.shape[0] // 2 for block in blocks]
    return call(
        halves_body,
        shape((sum(sizes), width)),
        *blocks,
        after=after,
        grid=(1,),
        in_specs=[pl.BlockSpec((size, width), lambda i: (1, 0)) for size in sizes],
        out_specs=pl.BlockSpec((sum(sizes), width), lambda i: (0, 0)),
        bytes_accessed=4 * sum(sizes) * width,
    )


def collect_body(column, count, adds, ends, *refs):
    slot_ref, held = refs[0], refs[-1]
    out = refs[-2]
    used = 2 if adds else 1
    blocks = refs[used : used + count]

    @pl.when(pl.program_id(0) == 0)
    def _():
        first = 0
        for ref in blocks:
            held[pl.ds(first, ref.shape[0]), :] = ref[...]
            first += ref.shape[0]

    slot = slot_ref[:, column : column + 1]
    place = lax.broadcasted_iota(jnp.int32, (slot.shape[0], held.shape[0]), 1)
    total = dot(jnp.where(place == slot, 1.0, 0.0).astype(BF16), held[...])
    if adds:
        total = total + refs[1][...].astype(F32)
    if ends:
        slope, w = refs[used + count], refs[used + count + 1]
        d_pre = (total * slope[...].astype(F32)).astype(BF16)
        out[...] = dot_nt(d_pre, w[...]).astype(BF16)
    else:
        out[...] = total.astype(BF16)


def collect(column, blocks, whole, slot_column, before=None, ends=()):
    blocks = list(blocks) + list(whole)
    rows, width = slot_column.shape[0], blocks[0].shape[1]
    step = 512
    part = pl.BlockSpec((step, width), lambda i: (i, 0))
    halved = len(blocks) - len(whole)
    sizes = [block.shape[0] // (2 if at < halved else 1) for at, block in enumerate(blocks)]
    prior = [] if before is None else [before]
    return call(
        functools.partial(collect_body, column, len(blocks), before is not None, bool(ends)),
        shape((rows, width)),
        slot_column,
        *prior,
        *blocks,
        *ends,
        grid=(rows // step,),
        in_specs=[pl.BlockSpec((step, slot_column.shape[1]), lambda i: (i, 0))]
        + [part] * len(prior)
        + [pl.BlockSpec((size, width), lambda i: (0, 0)) for size in sizes]
        + ([part, pl.BlockSpec((width, width), lambda i: (0, 0))] if ends else []),
        out_specs=part,
        scratch_shapes=[pltpu.VMEM((sum(sizes), width), BF16)],
        flops=2 * rows * sum(sizes) * width,
        bytes_accessed=4 * rows * width,
    )


def band_of(z, x, core):
    return (z % NZ) * 2 * NX + (x % NX) * 2 + core


def shift(value, dz=0, dx=0, dcore=0):
    pairs = [
        (band_of(z, x, core), band_of(z + dz, x + dx, core ^ dcore))
        for z in range(NZ)
        for x in range(NX)
        for core in range(2)
    ]
    return lax.ppermute(value, "band", pairs)


def along_patch(value, by):
    size = lax.axis_size("patch")
    return lax.ppermute(value, "patch", [(i, (i + by) % size) for i in range(size)])


def local(
    grid_feat, mesh_feat, grid_band, grid_target, mesh_nbr, w_in, w_mesh, w_edge, w_out, cotangent
):
    mesh_rows, width = mesh_feat.shape
    rows = grid_feat.shape[0]
    band = lax.axis_index("band")
    here = jnp.stack([band // (2 * NX), (band // 2) % NX, band % 2])
    named = jnp.stack([grid_band[:, 0], grid_target])
    other_named = shift(named, dcore=1)
    other_feat = shift(grid_feat, dcore=1)
    inside = pl.BlockSpec(memory_space=pltpu.VMEM)
    slot, table = call(
        index_body,
        [shape((16, rows), jnp.int32), shape((NX * NZ, 2 * CAP), F32)],
        here,
        named,
        other_named,
        in_specs=[pl.BlockSpec(memory_space=pltpu.SMEM), inside, inside],
    )
    slot_column = slot.T
    own, slope = message_of(grid_feat, w_in, 2)
    (other,) = message_of(other_feat, w_in, 1)

    span = jnp.arange(mesh_rows + 2 * HALO, dtype=jnp.int32)
    adjacency = jnp.zeros((mesh_rows, mesh_rows + 2 * HALO), F32)
    for column in range(mesh_nbr.shape[1]):
        adjacency = adjacency + (mesh_nbr[:, column : column + 1] == span[None, :]).astype(F32)
    adjacency = adjacency.astype(BF16)
    d_edge = dot(cotangent, w_out.T).astype(BF16)
    d_extended = lax.dot_general(
        adjacency, d_edge, (((0,), (0,)), ((), ())), preferred_element_type=F32
    )
    from_next = along_patch(d_extended[:HALO].astype(BF16), -1).astype(F32)
    from_prev = along_patch(d_extended[HALO + mesh_rows :].astype(BF16), 1).astype(F32)
    d_sender = d_extended[HALO : HALO + mesh_rows]
    d_sender = d_sender.at[:HALO].add(from_prev).at[mesh_rows - HALO :].add(from_next)

    def along_x(sent, way):
        return [sent[0]] + [shift(sent[k], dx=way * k) for k in range(1, NX)]

    sent = route(FAR, slot, own, other, table)
    arrived = along_x(sent, 1)
    sent_mid = route(MID, slot, own, other, after=(slot_column,))
    arrived_mid = along_x(sent_mid, 1)
    sent_near = route(NEAR, slot, own, other, after=(sent_mid[1],))
    arrived_near = along_x(sent_near, 1)
    three, four, five, listed, turned = merge(FAR, arrived, mesh_rows, after=(sent_near[1], d_extended))
    four, five = shift(four, dz=1), shift(five, dz=-1)
    three = shift(add(three, four), dz=1)
    two, six = merge(MID, arrived_mid, mesh_rows, listed, three, five)
    two, six = shift(two, dz=1), shift(six, dz=-1)
    up, down, near = merge(NEAR, arrived_near, mesh_rows, listed, two, six)
    up, down = shift(up, dz=1), shift(down, dz=-1)

    node = shape((mesh_rows, width))
    latent, sender, mesh_grad, mine = call(
        mesh_body,
        [node, node, node, node],
        near,
        up,
        down,
        mesh_feat,
        cotangent,
        d_sender,
        w_mesh,
        w_edge,
        flops=8 * mesh_rows * width * width,
        bytes_accessed=20 * mesh_rows * width,
    )

    before = along_patch(sender[mesh_rows - HALO :], 1)
    after = along_patch(sender[:HALO], -1)
    extended = jnp.concatenate([before, sender, after], axis=0)
    edge_total = dot(adjacency, extended).astype(BF16)
    mesh_out = (latent.astype(F32) + dot(edge_total, w_out)).astype(BF16)

    held = [mine] * NZ
    for k in range(1, NZ // 2 + 1):
        held[k] = shift(held[k - 1], dz=-1)
    for k in range(NZ - 1, NZ // 2, -1):
        held[k] = shift(held[(k + 1) % NZ], dz=1)
    arrived = along_x(expand(NEAR, turned, held, (mesh_out,)), -1)
    arrived += along_x(expand(MID, turned, held), -1)
    sent = expand(FAR, turned, held)
    swapped = shift(halves(arrived, (sent[0],)), dcore=1)
    total = collect(JOINED, arrived, (swapped,), slot_column)
    arrived = along_x(sent, -1)
    swapped = shift(halves(arrived, (total,)), dcore=1)
    total = collect(0, arrived, (), slot_column, total)
    grid_grad = collect(6, (), (swapped,), slot_column, total, (slope, w_in))
    return mesh_out, mesh_grad, grid_grad


def solution(mesh):
    spread = P(("band", "patch"), None)
    return jax.shard_map(
        local,
        mesh=mesh,
        in_specs=(
            spread,
            spread,
            spread,
            P(("band", "patch")),
            spread,
            P(),
            P(),
            P(),
            P(),
            spread,
        ),
        out_specs=(spread, spread, spread),
        check_vma=False,
    )
```
